256 devices in a mesh: span: 32 (over y, z), tp: 8 (over x, core).
Axes of the slice: x: 4, y: 4, z: 8, core: 2. Of those that a mesh axis runs over, the one named last changes fastest.
Arguments:
- latent: bfloat16 [16384, 5120], P(('span', 'tp')), may hold values from -6 to 6
- queries: bfloat16 [16384, 5120], P('span', 'tp'), may hold values from -8 to 8
- keys: bfloat16 [16384, 5120], P('span', 'tp'), may hold values from -8 to 8
- values: bfloat16 [16384, 5120], P('span', 'tp'), may hold values from -6 to 6
- out_weight: bfloat16 [5120, 5120], P('tp'), may hold values from -0.078125 to 0.078125
- level_gate: float32 [4, 5120], replicated, may hold values from 1 to 4
- levels: int32 [32], P('span'), may hold values from 0 to 3
- offset: int32 [1], replicated, may hold values from 0 to 31
- lag_mask: int32 [32, 7], P('span'), may hold values 0 or 1
- fresh_noise: bfloat16 [512, 5120], P('tp'), may hold values from -6 to 6
Outputs:
- next_latent: bfloat16 [16384, 5120], P(('span', 'tp'))
- released: bfloat16 [512, 5120], P('tp', 'span')
The draws below stay inside these ranges and needn't reach their ends.
All inputs are finite; a program needn't handle non-finite values. No bound on the sum of `lag_mask` on one device may be relied on, other than what follows from the above.
Results may differ from the reference program's by a relative error of at most 0.012.
Values may be sent and summed in bfloat16 or wider, within the bound.
A program may use at most 128 MiB of HBM per device.

```python
import jax
import jax.numpy as jnp
from jax import lax

D = 5120
HEADS = 40
HEAD_DIM = 128
ROWS = 512
LAGS = 7
LEVELS = 4
TOKENS = 16384
N_SPAN = 32
N_TP = 8


def draw_queries(key, part):
    key = jax.random.fold_in(key, 5)
    result = jnp.clip(1.6 * jax.random.normal(key, (TOKENS, D), jnp.float32), -8.0, 8.0)
    return result.astype(jnp.bfloat16)


def draw_keys(key, part):
    key = jax.random.fold_in(key, 9)
    result = jnp.clip(1.6 * jax.random.normal(key, (TOKENS, D), jnp.float32), -8.0, 8.0)
    return result.astype(jnp.bfloat16)


def with_ends(entries, rng, smallest, high):
    index_at = [jax.random.randint(jax.random.fold_in(rng, axis), (), 0, length) for axis, length in enumerate(entries.shape)]
    widest = entries.shape.index(max(entries.shape))
    next_to = index_at[:widest] + [(index_at[widest] + 1) % entries.shape[widest]] + index_at[widest + 1:]
    return entries.at[tuple(index_at)].set(smallest).at[tuple(next_to)].set(high)


def block_scale(rng, dims, cuts, least, top_value):
    gain, own = 1.0, jax.random.fold_in(rng, 6)
    for axis_at, shards_of in cuts:
        heights = jnp.exp(jax.random.uniform(jax.random.fold_in(own, axis_at), (shards_of,), jnp.float32, least / len(cuts), top_value / len(cuts)))
        gain = gain * jnp.repeat(heights, dims[axis_at] // shards_of).reshape([-1 if axis == axis_at else 1 for axis in range(len(dims))])
    return gain


def bell_draw(rng, dims, spread, bound, shards=(), held_as=jnp.bfloat16):
    values = jax.random.normal(rng, dims, jnp.float32) * spread
    if len(shards) > 0:
        values = block_scale(rng, dims, shards, -0.22, 0.18) * values
    return jnp.clip(values, min=-bound, max=bound).astype(held_as)


def setup_inputs(seed: int = 0) -> dict:
    key_list = jax.random.split(jax.random.key(seed), 11)
    latent = bell_draw(key_list[0], (TOKENS, D), 1.0, 6.0, ((0, 256),))
    queries = draw_queries(jax.random.fold_in(key_list[10], 71), 0)
    keys = draw_keys(jax.random.fold_in(key_list[10], 71), 0)
    values = bell_draw(key_list[3], (TOKENS, D), 1.0, 6.0, ((0, 32), (1, 8)))
    out_weight = bell_draw(key_list[4], (D, D), D ** -0.5, 0.078125, ((0, 8),))
    level_gate = jnp.clip(jax.random.uniform(key_list[5], (LEVELS, D), jnp.float32, 1.0, 4.0), 1.0, 4.0)
    levels = with_ends(jax.random.randint(key_list[6], (N_SPAN,), 0, LEVELS), jax.random.fold_in(key_list[6], 1), 0, LEVELS - 1).astype(jnp.int32)
    offset = jax.random.randint(key_list[7], (1,), 0, N_SPAN).astype(jnp.int32)
    lag_mask = with_ends((jax.random.randint(key_list[8], (N_SPAN, LAGS), 0, 4) < 3).astype(jnp.int32), jax.random.fold_in(key_list[8], 1), 0, 1)
    fresh_noise = bell_draw(key_list[9], (ROWS, D), 1.0, 6.0, ((0, 8),))
    return {"latent": latent, "queries": queries, "keys": keys, "values": values, "out_weight": out_weight, "level_gate": level_gate, "levels": levels, "offset": offset, "lag_mask": lag_mask, "fresh_noise": fresh_noise}


def attend_head(operands, usable):
    query, key_blocks, value_blocks = operands
    scores = jnp.einsum("qd,lkd->lqk", query.astype(jnp.float32), key_blocks.astype(jnp.float32)) * (HEAD_DIM ** -0.5)
    scores = jnp.where(usable[:, None, None], scores, -jnp.inf)
    row_peak = jnp.max(scores, axis=(0, 2))
    weights = jnp.exp(scores - row_peak[None, :, None])
    row_total = jnp.sum(weights, axis=(0, 2))
    rounded = lax.optimization_barrier(weights.astype(jnp.bfloat16))
    weighted = jnp.einsum("lqk,lkd->qd", rounded.astype(jnp.float32), value_blocks.astype(jnp.float32))
    return (weighted / row_total[:, None]).astype(jnp.bfloat16)


def reference(latent, queries, keys, values, out_weight, level_gate, levels, offset, lag_mask, fresh_noise):
    query_all = queries.reshape(N_SPAN, ROWS, HEADS, HEAD_DIM)
    key_all = keys.reshape(N_SPAN, ROWS, HEADS, HEAD_DIM)
    value_all = values.reshape(N_SPAN, ROWS, HEADS, HEAD_DIM)
    lag_steps = jnp.arange(1, LAGS + 1, dtype=jnp.int32)

    def one_slot(slot_index):
        position = (slot_index - offset[0]) % N_SPAN
        usable = jnp.concatenate([jnp.ones((1,), jnp.bool_), (lag_mask[slot_index] == 1) & (position >= lag_steps)])
        sources = (slot_index - jnp.arange(LAGS + 1, dtype=jnp.int32)) % N_SPAN
        key_blocks = jnp.take(key_all, sources, axis=0).transpose(2, 0, 1, 3)
        value_blocks = jnp.take(value_all, sources, axis=0).transpose(2, 0, 1, 3)
        query_heads = query_all[slot_index].transpose(1, 0, 2)
        heads_out = lax.map(lambda operands: attend_head(operands, usable), (query_heads, key_blocks, value_blocks))
        return heads_out.transpose(1, 0, 2).reshape(ROWS, D)

    attended = lax.map(one_slot, jnp.arange(N_SPAN, dtype=jnp.int32)).reshape(N_SPAN * ROWS, D)
    group_width = D // N_TP
    attended_groups = attended.reshape(N_SPAN * ROWS, N_TP, group_width).transpose(1, 0, 2)
    weight_groups = out_weight.reshape(N_TP, group_width, D)

    def group_partial(operands):
        left, right = operands
        return jnp.dot(left, right, preferred_element_type=jnp.float32).astype(jnp.bfloat16)

    partials = lax.map(group_partial, (attended_groups, weight_groups))
    summed = jnp.sum(partials.astype(jnp.float32), axis=0)
    gate_rows = jnp.repeat(jnp.take(level_gate, levels, axis=0), ROWS, axis=0)
    updated = (latent.astype(jnp.float32) - gate_rows * summed / LEVELS).astype(jnp.bfloat16)
    per_slot = updated.reshape(N_SPAN, ROWS, D)
    released = lax.dynamic_index_in_dim(per_slot, offset[0], 0, keepdims=False)
    is_oldest = jnp.arange(N_SPAN, dtype=jnp.int32) == offset[0]
    next_latent = jnp.where(is_oldest[:, None, None], fresh_noise[None], per_slot).reshape(N_SPAN * ROWS, D)
    return next_latent, released
```

```python
import functools

import jax
import jax.numpy as jnp
from jax import lax
from jax.experimental import pallas as pl
from jax.experimental.pallas import tpu as pltpu
from jax.sharding import PartitionSpec as P

MESH = pl.DeviceIdType.MESH
HD = 128
ROWS = 512
WIDTH = 640
D = 5120
NY, NZ, NX = 4, 8, 4
SLOTS = NY * NZ
LAGS = 7
CHUNKS = 2
CROWS = 64 // CHUNKS
M = NX * CROWS
ITEMS = 10
N_ITEMS = CHUNKS * ITEMS
FAR = -1e30
SCALE2 = HD ** -0.5 * 1.4426950408889634
COLS = 1024
PARTS = D // COLS
NT = (((1,), (1,)), ((), ()))
ORDER = (0, 1, 7, 2, 6, 3, 5, 4)


def lanes(col, width):
    return jnp.concatenate([col] * (width // HD), axis=1)


def fold_max(x):
    return jnp.maximum(
        jnp.maximum(x[:, :128], x[:, 128:256]), jnp.maximum(x[:, 256:384], x[:, 384:])
    )


def fold_sum(x):
    return (x[:, :128] + x[:, 128:256]) + (x[:, 256:384] + x[:, 384:])


def kernel(
    latent_ref, q_ref, k_ref, v_ref, w_ref, gate_ref, levels_ref, offset_ref, mask_ref,
    fresh_ref, out_ref, rel_ref,
    wb, kv, qd, bias_all, os, a1, qv, kvv, vvv, o0, a0, s0, r0, s1, r1, u0, ry, u1, rz,
    lat, fre, gate_row, bias_own, sca, scb, ma, mb,
    load_sem, kv_ss, kv_rs, rel_ss, rel_rs, q_ss, q_rs, b_ss, b_rs, w_ss, w_rs,
    ft_ss, ft_rs, fy_ss, fy_rs, fty_ss, fty_rs, o0_sem, x0_ss, x0_rs, o_ss, o_rs,
    x1_ss, x1_rs, y_ss, y_rs, z_ss, z_rs,
):
    me = lax.axis_index("span")
    t = lax.axis_index("tp")
    y, z = me // NZ, me % NZ
    x, c = t // 2, t % 2
    twin_c = 1 - c

    def at(yy, zz, xx, cc):
        return (lax.rem(yy + NY, NY) * NZ + lax.rem(zz + NZ, NZ), lax.rem(xx + NX, NX) * 2 + cc)

    def slot_dev(shift):
        return (lax.rem(me + shift + SLOTS, SLOTS), t)

    twin = at(y, z, x, twin_c)

    def remote(src, dst, ss, rs, dev):
        return pltpu.make_async_remote_copy(
            src_ref=src, dst_ref=dst, send_sem=ss, recv_sem=rs, device_id=dev,
            device_id_type=MESH,
        )

    loads = [
        pltpu.make_async_copy(q_ref, qv, load_sem.at[0]),
        pltpu.make_async_copy(k_ref, kvv, load_sem.at[1]),
        pltpu.make_async_copy(v_ref, vvv, load_sem.at[2]),
        pltpu.make_async_copy(k_ref.at[:, pl.ds(512, 128)], kv.at[23, 0], load_sem.at[3]),
        pltpu.make_async_copy(v_ref.at[:, pl.ds(512, 128)], kv.at[23, 1], load_sem.at[4]),
        pltpu.make_async_copy(
            w_ref, wb.at[pl.ds(pl.multiple_of(c * WIDTH, 128), WIDTH)], load_sem.at[5]
        ),
        pltpu.make_async_copy(latent_ref, lat, load_sem.at[6]),
        pltpu.make_async_copy(fresh_ref, fre, load_sem.at[7]),
    ]
    for copy in loads:
        copy.start()
    q_loads = []
    for k in range(CHUNKS):
        for p in range(2):
            q_loads.append(
                pltpu.make_async_copy(
                    q_ref.at[:, p, pl.ds(CROWS * k, CROWS), pl.ds(512, 128)],
                    qd.at[k, 8 + p], load_sem.at[8 + 2 * k + p],
                )
            )
            q_loads[-1].start()

    barrier = pltpu.get_barrier_semaphore()
    partners = [twin]
    for dz in range(1, NZ):
        partners += [at(y, z + dz, x, c), at(y, z + dz, x, twin_c)]
    for dy in range(1, NY):
        partners.append(at(y + dy, z, x, c))
    for dx in range(1, NX):
        partners.append(at(y, z, x + dx, c))
    for shift in (1, -1, 7, -7):
        partners.append(slot_dev(shift))
    for dev in partners:
        pl.semaphore_signal(barrier, inc=1, device_id=dev, device_id_type=MESH)
    pl.semaphore_wait(barrier, len(partners))

    position = lax.rem(me - offset_ref[0] + SLOTS, SLOTS)
    lag_at = lax.broadcasted_iota(jnp.int32, (8, 128), 0)
    bias = jnp.zeros((8, 128), jnp.float32)
    for lag in range(1, LAGS + 1):
        ok = (mask_ref[0, lag - 1] == 1) & (position >= lag)
        bias = jnp.where(lag_at == lag, jnp.where(ok, 0.0, FAR), bias)
    bias_own[...] = bias
    bias_all[8] = bias
    bias_all[9] = bias
    level = levels_ref[0]
    row = gate_ref[0:1, :]
    for i in range(1, 4):
        row = jnp.where(level == i, gate_ref[i : i + 1, :], row)
    gate_row[...] = row * 0.25

    def kv_send(j, hf, which):
        ref = (k_ref, v_ref)[which]
        src = ref.at[pl.ds(256 * hf, 256), pl.ds(128 * j, 128)]
        dst = kv.at[8 + z, which, pl.ds(256 * hf, 256)]
        d = 4 * c + j
        return src, dst, kv_ss.at[j, hf, which], kv_rs.at[z, which], d, hf

    def q_send(j, hf, k):
        src = q_ref.at[:, hf, pl.ds(CROWS * k, CROWS), pl.ds(128 * j, 128)]
        dst = qd.at[k, z]
        return src, dst, q_ss.at[j, hf, k], q_rs.at[k, z], 4 * c + j, hf

    def b_send(j, hf):
        return bias_own, bias_all.at[z], b_ss.at[j, hf], b_rs.at[z], 4 * c + j, hf

    def go(args):
        src, dst, ss, rs, d, hf = args
        mine = (d == z) & (c == hf)

        @pl.when(mine)
        def _():
            pltpu.make_async_copy(src, dst, rs).start()

        @pl.when(jnp.logical_not(mine))
        def _():
            remote(src, dst, ss, rs, at(y, d, x, hf)).start()

    def gone(args):
        src, dst, ss, rs, d, hf = args

        @pl.when(jnp.logical_not((d == z) & (c == hf)))
        def _():
            remote(src, dst, ss, rs, at(y, d, x, hf)).wait_send()

    def lag_slot(lag):
        return 16 + 7 - lag

    def relay_first(which, ahead):
        ref = (k_ref, v_ref)[which]
        return remote(
            ref.at[:, pl.ds(512, 128)], kv.at[lag_slot(7 if ahead else 1), which],
            rel_ss.at[ahead, which], rel_rs.at[ahead, which],
            slot_dev(7 if ahead else 1),
        )

    def relay_next(step, ahead):
        old, new = (8 - step, 7 - step) if ahead else (step, step + 1)
        part = pl.ds(0, 512) if step < 3 else pl.ds(256 * ahead, 256)
        return remote(
            kv.at[lag_slot(old), :, part], kv.at[lag_slot(new), :, part],
            rel_ss.at[ahead, 1 + step], rel_rs.at[ahead, 1 + step],
            slot_dev(-1 if ahead else 1),
        )

    for which in range(2):
        for j in range(4):
            for hf in range(2):
                go(kv_send(j, hf, which))
    for ahead in range(2):
        for which in range(2):
            relay_first(which, ahead).start()
    for j in range(4):
        for hf in range(2):
            go(b_send(j, hf))
    w_send = remote(
        w_ref, wb.at[pl.ds(pl.multiple_of(c * WIDTH, 128), WIDTH)], w_ss.at[0], w_rs.at[0], twin
    )
    w_send.start()
    for k in range(CHUNKS):
        for j in range(4):
            for hf in range(2):
                go(q_send(j, hf, k))

    for copy in loads[:3]:
        copy.wait()

    def head_at_home(i, carry):
        head, half = i // 2, i % 2
        col = pl.ds(pl.multiple_of(head * 128, 128), 128)
        q = qv[pl.ds(2 * half, 2), :, :, col].reshape(256, HD)
        s = lax.dot_general(q, kvv[:, col], NT, preferred_element_type=jnp.float32)
        top = jnp.max(fold_max(s), axis=1, keepdims=True) * SCALE2
        p = jnp.exp2(s * SCALE2 - top)
        total = jnp.sum(fold_sum(p), axis=1, keepdims=True)
        o = jnp.dot(p.astype(jnp.bfloat16), vvv[:, col], preferred_element_type=jnp.float32)
        o0[pl.ds(2 * half, 2), :, :, col] = (
            (o / total).astype(jnp.bfloat16).reshape(2, 2, 64, HD)
        )
        return carry

    lax.fori_loop(0, 10, head_at_home, 0)
    own_cols = pl.ds(pl.multiple_of(c * WIDTH, 128), WIDTH)
    o0_own = pltpu.make_async_copy(o0.at[:, c], a0.at[:, :, own_cols], o0_sem.at[0])
    o0_twin = remote(
        o0.at[:, twin_c], a0.at[:, :, own_cols], o0_sem.at[1], o0_sem.at[2], twin
    )
    o0_own.start()
    o0_twin.start()

    half = pl.ds(pl.multiple_of(256 * c, 256), 256)
    other = pl.ds(pl.multiple_of(256 * twin_c, 256), 256)

    def to_twin(src_z):
        ref = kv.at[8 + src_z, :, half]
        return remote(ref, ref, ft_ss.at[src_z], ft_rs.at[src_z], twin)

    def to_next(src_z):
        return remote(
            kv.at[8 + src_z, :, half], kv.at[src_z, :, half], fy_ss.at[src_z],
            fy_rs.at[src_z], at(y + 1, z, x, c),
        )

    def prev_to_twin(src_z):
        ref = kv.at[src_z, :, half]
        return remote(ref, ref, fty_ss.at[src_z], fty_rs.at[src_z], twin)

    def pass_on(shift):
        src_z = lax.rem(z + shift, NZ)
        for which in range(2):
            ref = kv.at[8 + src_z, which, half]
            pltpu.make_async_copy(ref, ref, kv_rs.at[src_z, which]).wait()
        to_next(src_z).start()
        to_twin(src_z).start()

    def pass_prev(shift):
        src_z = lax.rem(z + shift, NZ)
        to_next(src_z).wait_recv()
        prev_to_twin(src_z).start()

    def project(a_ref, s_ref, r_ref, rows, ss, rs):
        def part(n, carry):
            for h in range(2):
                col = pl.ds(pl.multiple_of(n * COLS + h * 512, 512), 512)
                a = a_ref[...].reshape(NX * rows, 2 * WIDTH)
                out = jnp.dot(a, wb[:, col], preferred_element_type=jnp.float32)
                s_ref[:, :, col] = out.astype(jnp.bfloat16).reshape(NX, rows, 512)
            for dx in range(1, NX):
                x_send(s_ref, r_ref, ss, rs, n, dx).start()
            return carry

        lax.fori_loop(0, PARTS, part, 0)

    def x_send(s_ref, r_ref, ss, rs, n, dx):
        col = pl.ds(pl.multiple_of(n * COLS, COLS), COLS)
        to_x = lax.rem(x + dx, NX)
        return remote(
            s_ref.at[to_x, :, col], r_ref.at[3 - dx, :, col], ss.at[n, dx - 1],
            rs.at[n, 3 - dx], at(y, z, to_x, c),
        )

    def gather_x(s_ref, r_ref, ss, rs, n, lat_rows, write):
        for dx in range(1, NX):
            x_send(s_ref, r_ref, ss, rs, n, dx).wait_recv()
        for h in range(2):
            col = pl.ds(pl.multiple_of(n * COLS + h * 512, 512), 512)
            total = s_ref[x, :, col].astype(jnp.float32)
            for i in range(3):
                total = total + r_ref[i, :, col].astype(jnp.float32)
            updated = lat[lat_rows, col].astype(jnp.float32) - gate_row[:, col] * total
            write(col, updated.astype(jnp.bfloat16))

    def sent_x(s_ref, r_ref, ss, rs):
        def part(n, carry):
            for dx in range(1, NX):
                x_send(s_ref, r_ref, ss, rs, n, dx).wait_send()
            return carry

        lax.fori_loop(0, PARTS, part, 0)

    pass_on(0)
    pass_on(1)
    pass_on(7)
    for ahead in range(2):
        for which in range(2):
            relay_first(which, ahead).wait_recv()
        relay_next(1, ahead).start()

    for copy in loads[5:]:
        copy.wait()
    w_send.wait_recv()
    o0_own.wait()
    o0_twin.wait_recv()
    project(a0, s0, r0, 64, x0_ss, x0_rs)

    pass_on(2)
    pass_on(6)
    for shift in (0, 1, 7):
        pass_prev(shift)
    for ahead in range(2):
        relay_next(1, ahead).wait_recv()
        relay_next(2, ahead).start()
    pass_on(3)
    pass_on(5)
    pass_on(4)

    oldest = position == 0

    def write_u0(col, updated):
        u0[:, col] = jnp.where(oldest, updated, jnp.zeros_like(updated))

    def finish0(n, carry):
        gather_x(s0, r0, x0_ss, x0_rs, n, slice(None), write_u0)
        return carry

    for ahead in range(2):
        relay_next(2, ahead).wait_recv()
        relay_next(3, ahead).start()
    for shift in (2, 6, 3, 5, 4):
        pass_prev(shift)

    lax.fori_loop(0, PARTS, finish0, 0)
    y_width = D // NY

    def y_send(dy):
        to_y = lax.rem(y + dy, NY)
        return remote(
            u0.at[:, pl.ds(pl.multiple_of(to_y * y_width, 128), y_width)], ry.at[3 - dy],
            y_ss.at[dy - 1], y_rs.at[3 - dy], at(to_y, z, x, c),
        )

    for dy in range(1, NY):
        y_send(dy).start()

    def z_window(zz):
        return pl.ds(pl.multiple_of((zz * 160 // 128) * 128, 128), 256)

    def z_send(dz):
        to_z = lax.rem(z + dz, NZ)
        return remote(
            u1.at[:, z_window(to_z)], rz.at[7 - dz], z_ss.at[dz - 1], z_rs.at[7 - dz],
            at(y, to_z, x, c),
        )

    def share_y():
        for dy in range(1, NY):
            y_send(dy).wait_recv()
        total = u0[:, pl.ds(pl.multiple_of(y * y_width, 128), y_width)].astype(jnp.float32)
        for i in range(3):
            total = total + ry[i].astype(jnp.float32)
        u1[...] = total.astype(jnp.bfloat16)
        for dz in range(1, NZ):
            z_send(dz).start()

    def share_z():
        for dz in range(1, NZ):
            z_send(dz).wait_recv()
        total = u1[:, z_window(z)].astype(jnp.float32)
        for i in range(7):
            total = total + rz[i].astype(jnp.float32)
        turned = pltpu.roll(total, lax.rem(256 - (z % 4) * 32, 256), 1)
        rel_ref[...] = turned[:, :160].astype(jnp.bfloat16)

    for copy in loads[3:5] + q_loads:
        copy.wait()
    for ahead in range(2):
        relay_next(3, ahead).wait_recv()
    for src_z in range(NZ):
        to_twin(src_z).wait_recv()
        prev_to_twin(src_z).wait_recv()

    def item(it):
        k, j = it // ITEMS, it % ITEMS
        off = jnp.where(j % 2 == 1, (j + 1) // 2, NZ - j // 2)
        s = jnp.where(j < 8, lax.rem(z + off, NZ), j)
        return k, j, s, jnp.where(j < 8, s + 1, 16)

    def o_send(it):
        k, j, s, _ = item(it)
        gathered = j < 8
        to_z = jnp.where(gathered, s, z)
        to_c = jnp.where(gathered, c, j - 8)
        head_col = jnp.where(gathered, (z // 4) * WIDTH + (z % 4) * HD, c * WIDTH + 4 * HD)
        dst = a1.at[k, :, :, pl.ds(pl.multiple_of(head_col, 128), 128)]
        rs = o_rs.at[k, jnp.where(gathered, z, 8 + c)]
        return os.at[k, s], dst, o_ss.at[k, s], rs, to_z, to_c

    def arrived(it):
        k, j, s, _ = item(it)

        @pl.when(j < 8)
        def _():
            pltpu.make_async_copy(qd.at[k, s], qd.at[k, s], q_rs.at[k, s]).wait()

        @pl.when((j < 8) & (k == 0))
        def _():
            pltpu.make_async_copy(bias_all.at[s], bias_all.at[s], b_rs.at[s]).wait()

    def first_pass(q, s, base, i, sc, top):
        scores = lax.dot_general(q, kv[base + i, 0], NT, preferred_element_type=jnp.float32)
        sc[i] = scores
        return jnp.maximum(top, fold_max(scores) * SCALE2 + bias_all[s, 7 - i : 8 - i, :])

    def second_pass(s, base, i, sc, top, total, acc):
        p = jnp.exp2(sc[i] * SCALE2 - lanes(top - bias_all[s, 7 - i : 8 - i, :], 512))
        acc = acc + jnp.dot(
            p.astype(jnp.bfloat16), kv[base + i, 1], preferred_element_type=jnp.float32
        )
        return total + fold_sum(p), acc

    def row_top(top):
        return jnp.broadcast_to(jnp.max(top, axis=1, keepdims=True), (M, HD))

    def stage(it, sc, m_ref, next_sc, next_m, last=False):
        k, j, s, base = item(it)
        if not last:
            arrived(it + 1)
            k2, _, s2, base2 = item(it + 1)
            q = qd[k2, s2].reshape(M, HD)
        top = m_ref[...]
        next_top = jnp.full((M, HD), FAR, jnp.float32)
        total = jnp.zeros((M, HD), jnp.float32)
        acc = jnp.zeros((M, HD), jnp.float32)
        for i in range(8):
            if not last:
                next_top = first_pass(q, s2, base2, i, next_sc, next_top)
            total, acc = second_pass(s, base, i, sc, top, total, acc)
        if not last:
            next_m[...] = row_top(next_top)
        o = acc / jnp.sum(total, axis=1, keepdims=True)
        os[k, s] = o.astype(jnp.bfloat16).reshape(NX, CROWS, HD)
        src, dst, ss, rs, to_z, to_c = o_send(it)
        mine = (to_z == z) & (to_c == c)

        @pl.when(mine)
        def _():
            pltpu.make_async_copy(src, dst, rs).start()

        @pl.when(jnp.logical_not(mine))
        def _():
            remote(src, dst, ss, rs, at(y, to_z, x, to_c)).start()

    def project_chunk(k):
        for h in range(10):
            ref = a1.at[k, :, :, pl.ds(0, 128)]
            pltpu.make_async_copy(ref, ref, o_rs.at[k, h]).wait()
        project(a1.at[k], s1.at[k], r1.at[k], CROWS, x1_ss.at[k], x1_rs.at[k])

    arrived(0)
    k, _, s, base = item(0)
    q = qd[k, s].reshape(M, HD)
    top = jnp.full((M, HD), FAR, jnp.float32)
    for i in range(8):
        top = first_pass(q, s, base, i, sca, top)
    ma[...] = row_top(top)

    def pair(j, carry):
        stage(2 * j, sca, ma, scb, mb)

        @pl.when(j < N_ITEMS // 2 - 1)
        def _():
            stage(2 * j + 1, scb, mb, sca, ma)

        @pl.when(j == 1)
        def _():
            share_y()

        @pl.when(j == 3)
        def _():
            share_z()

        @pl.when(j == 6)
        def _():
            project_chunk(0)

        return carry

    lax.fori_loop(0, N_ITEMS // 2, pair, 0)
    stage(N_ITEMS - 1, scb, mb, sca, ma, last=True)
    project_chunk(1)

    def finish(k):
        rows = pl.ds(CROWS * k, CROWS)

        def write(col, updated):
            out_ref[rows, col] = jnp.where(oldest, fre[rows, col], updated)

        def part(n, carry):
            gather_x(s1.at[k], r1.at[k], x1_ss.at[k], x1_rs.at[k], n, rows, write)
            return carry

        lax.fori_loop(0, PARTS, part, 0)

    finish(0)
    finish(1)

    for which in range(2):
        for j in range(4):
            for hf in range(2):
                gone(kv_send(j, hf, which))
    for ahead in range(2):
        for which in range(2):
            relay_first(which, ahead).wait_send()
        for step in range(1, 4):
            relay_next(step, ahead).wait_send()
    for j in range(4):
        for hf in range(2):
            gone(b_send(j, hf))
            for k in range(CHUNKS):
                gone(q_send(j, hf, k))
    w_send.wait_send()
    o0_twin.wait_send()
    for src_z in range(NZ):
        to_twin(src_z).wait_send()
        to_next(src_z).wait_send()
        prev_to_twin(src_z).wait_send()
    sent_x(s0, r0, x0_ss, x0_rs)
    for k in range(CHUNKS):
        sent_x(s1.at[k], r1.at[k], x1_ss.at[k], x1_rs.at[k])
    for dy in range(1, NY):
        y_send(dy).wait_send()
    for dz in range(1, NZ):
        z_send(dz).wait_send()

    def o_gone(it, carry):
        src, dst, ss, rs, to_z, to_c = o_send(it)

        @pl.when(jnp.logical_not((to_z == z) & (to_c == c)))
        def _():
            remote(src, dst, ss, rs, at(y, to_z, x, to_c)).wait_send()

        return carry

    lax.fori_loop(0, N_ITEMS, o_gone, 0)


def body(
    latent, queries, keys, values, out_weight, level_gate, levels, offset, lag_mask, fresh_noise
):
    bf16, f32 = jnp.bfloat16, jnp.float32
    hbm = pl.BlockSpec(memory_space=pl.ANY)
    vmem = pl.BlockSpec(memory_space=pltpu.VMEM)
    smem = pl.BlockSpec(memory_space=pltpu.SMEM)
    dma = pltpu.SemaphoreType.DMA
    vm = pltpu.VMEM
    scratch = [
        vm((2 * WIDTH, D), bf16),
        vm((24, 2, ROWS, HD), bf16),
        vm((CHUNKS, ITEMS, NX, CROWS, HD), bf16),
        vm((ITEMS, 8, 128), f32),
        vm((CHUNKS, ITEMS, NX, CROWS, HD), bf16),
        vm((CHUNKS, NX, CROWS, 2 * WIDTH), bf16),
        vm((NX, 2, 64, WIDTH), bf16),
        vm((ROWS, WIDTH), bf16),
        vm((ROWS, WIDTH), bf16),
        vm((NX, 2, 64, WIDTH), bf16),
        vm((NX, 64, 2 * WIDTH), bf16),
        vm((NX, 64, D), bf16),
        vm((NX - 1, 64, D), bf16),
        vm((CHUNKS, NX, CROWS, D), bf16),
        vm((CHUNKS, NX - 1, CROWS, D), bf16),
        vm((64, D), bf16),
        vm((NY - 1, 64, D // NY), bf16),
        vm((64, D // NY), bf16),
        vm((NZ - 1, 64, 256), bf16),
        vm((64, D), bf16),
        vm((64, D), bf16),
        vm((1, D), f32),
        vm((8, 128), f32),
        vm((8, M, ROWS), f32),
        vm((8, M, ROWS), f32),
        vm((M, HD), f32),
        vm((M, HD), f32),
        dma((8 + 2 * CHUNKS,)),
        dma((4, 2, 2)), dma((NZ, 2)),
        dma((2, 5)), dma((2, 5)),
        dma((4, 2, CHUNKS)), dma((CHUNKS, NZ)),
        dma((4, 2)), dma((NZ,)),
        dma((1,)), dma((1,)),
        dma((NZ,)), dma((NZ,)),
        dma((NZ,)), dma((NZ,)),
        dma((NZ,)), dma((NZ,)),
        dma((3,)),
        dma((PARTS, 3)), dma((PARTS, 3)),
        dma((CHUNKS, ITEMS)), dma((CHUNKS, ITEMS)),
        dma((CHUNKS, PARTS, 3)), dma((CHUNKS, PARTS, 3)),
        dma((3,)), dma((3,)),
        dma((7,)), dma((7,)),
    ]
    return pl.pallas_call(
        kernel,
        out_shape=(
            jax.ShapeDtypeStruct((64, D), bf16),
            jax.ShapeDtypeStruct((64, 160), bf16),
        ),
        in_specs=[hbm, hbm, hbm, hbm, hbm, vmem, smem, smem, smem, hbm],
        out_specs=(vmem, vmem),
        scratch_shapes=scratch,
        compiler_params=pltpu.CompilerParams(
            collective_id=1, has_side_effects=True, vmem_limit_bytes=56 << 20
        ),
        name="window_step",
    )(
        latent, queries.reshape(NX, 2, 64, WIDTH), keys, values, out_weight, level_gate,
        levels, offset, lag_mask, fresh_noise,
    )


def solution(mesh):
    return jax.shard_map(
        body,
        mesh=mesh,
        in_specs=(
            P(("span", "tp"), None),
            P("span", "tp"),
            P("span", "tp"),
            P("span", "tp"),
            P("tp", None),
            P(),
            P("span"),
            P(),
            P("span", None),
            P("tp", None),
        ),
        out_specs=(P(("span", "tp"), None), P("tp", "span")),
        check_vma=False,
    )
```

```python
import functools

import jax
import jax.numpy as jnp
from jax import lax
from jax.experimental import pallas as pl
from jax.experimental.pallas import tpu as pltpu
from jax.sharding import PartitionSpec as P

MESH = pl.DeviceIdType.MESH
HD = 128
ROWS = 512
WIDTH = 640
D = 5120
NY, NZ, NX = 4, 8, 4
SLOTS = NY * NZ
LAGS = 7
CHUNKS = 2
CROWS = 64 // CHUNKS
M = NX * CROWS
ITEMS = 10
N_ITEMS = CHUNKS * ITEMS
FAR = -1e30
SCALE2 = HD ** -0.5 * 1.4426950408889634
COLS = 1024
PARTS = D // COLS
NT = (((1,), (1,)), ((), ()))
FIRST_STAY = 12
PLAN = {1: ("r3",), 5: ("fr",), 7: ("p0",)}


def lanes(col, width):
    return jnp.concatenate([col] * (width // HD), axis=1)


def fold_max(x):
    return jnp.maximum(
        jnp.maximum(x[:, :128], x[:, 128:256]), jnp.maximum(x[:, 256:384], x[:, 384:])
    )


def fold_sum(x):
    return (x[:, :128] + x[:, 128:256]) + (x[:, 256:384] + x[:, 384:])


def kernel(
    latent_ref, q_ref, k_ref, v_ref, w_ref, gate_ref, levels_ref, offset_ref, mask_ref,
    fresh_ref, out_ref, rel_ref,
    wb, kv, qd, bias_all, os, a1, qv, kvv, vvv, o0, a0, s0, r0, s1, r1, u0, ry, u1, rz,
    new, lat, fre, gate_row, bias_own, sca, scb, ma, mb,
    load_sem, kv_ss, kv_rs, rel_ss, rel_rs, q_ss, q_rs, b_ss, b_rs, w_ss, w_rs,
    ft_ss, ft_rs, fy_ss, fy_rs, fty_ss, fty_rs, o0_sem, x0_ss, x0_rs, o_ss, o_rs,
    x1_ss, x1_rs, out_sem, y_ss, y_rs, z_ss, z_rs,
):
    me = lax.axis_index("span")
    t = lax.axis_index("tp")
    y, z = me // NZ, me % NZ
    x, c = t // 2, t % 2
    twin_c = 1 - c

    def at(yy, zz, xx, cc):
        return (lax.rem(yy + NY, NY) * NZ + lax.rem(zz + NZ, NZ), lax.rem(xx + NX, NX) * 2 + cc)

    def slot_dev(shift):
        return (lax.rem(me + shift + SLOTS, SLOTS), t)

    twin = at(y, z, x, twin_c)

    def remote(src, dst, ss, rs, dev):
        return pltpu.make_async_remote_copy(
            src_ref=src, dst_ref=dst, send_sem=ss, recv_sem=rs, device_id=dev,
            device_id_type=MESH,
        )

    def settle(ref, sem):
        pltpu.make_async_copy(ref, ref, sem).wait()

    loads = [
        pltpu.make_async_copy(q_ref, qv, load_sem.at[0]),
        pltpu.make_async_copy(k_ref, kvv, load_sem.at[1]),
        pltpu.make_async_copy(v_ref, vvv, load_sem.at[2]),
        pltpu.make_async_copy(k_ref.at[:, pl.ds(512, 128)], kv.at[23, 0], load_sem.at[3]),
        pltpu.make_async_copy(v_ref.at[:, pl.ds(512, 128)], kv.at[23, 1], load_sem.at[3]),
        pltpu.make_async_copy(
            w_ref, wb.at[pl.ds(pl.multiple_of(c * WIDTH, 128), WIDTH)], load_sem.at[5]
        ),
        pltpu.make_async_copy(latent_ref, lat, load_sem.at[6]),
        pltpu.make_async_copy(fresh_ref, fre, load_sem.at[7]),
    ]
    for copy in loads:
        copy.start()
    q_loads = []
    for k in range(CHUNKS):
        for p in range(2):
            q_loads.append(
                pltpu.make_async_copy(
                    q_ref.at[:, p, pl.ds(CROWS * k, CROWS), pl.ds(512, 128)],
                    qd.at[k, 8 + p], load_sem.at[4],
                )
            )
            q_loads[-1].start()

    barrier = pltpu.get_barrier_semaphore()
    partners = [twin]
    for dz in range(1, NZ):
        partners += [at(y, z + dz, x, c), at(y, z + dz, x, twin_c)]
    for dy in range(1, NY):
        partners.append(at(y + dy, z, x, c))
    for dx in range(1, NX):
        partners.append(at(y, z, x + dx, c))
    for shift in (1, -1, 7, -7):
        partners.append(slot_dev(shift))
    for dev in partners:
        pl.semaphore_signal(barrier, inc=1, device_id=dev, device_id_type=MESH)
    pl.semaphore_wait(barrier, len(partners))

    position = lax.rem(me - offset_ref[0] + SLOTS, SLOTS)
    lag_at = lax.broadcasted_iota(jnp.int32, (8, 128), 0)
    bias = jnp.zeros((8, 128), jnp.float32)
    for lag in range(1, LAGS + 1):
        ok = (mask_ref[0, lag - 1] == 1) & (position >= lag)
        bias = jnp.where(lag_at == lag, jnp.where(ok, 0.0, FAR), bias)
    bias_own[...] = bias
    bias_all[8] = bias
    bias_all[9] = bias
    level = levels_ref[0]
    row = gate_ref[0:1, :]
    for i in range(1, 4):
        row = jnp.where(level == i, gate_ref[i : i + 1, :], row)
    gate_row[...] = row * 0.25

    def turned(i):
        return lax.rem(z + i, 4)

    def head_cols(j):
        return pl.ds(pl.multiple_of(128 * j, 128), 128)

    def kv_send(i, hf, which):
        j = turned(i)
        ref = (k_ref, v_ref)[which]
        src = ref.at[pl.ds(256 * hf, 256), head_cols(j)]
        dst = kv.at[8 + z, which, pl.ds(256 * hf, 256)]
        d = 4 * c + j
        return src, dst, kv_ss.at[0], kv_rs.at[z], d, hf

    def q_send(i, hf, k):
        j = turned(i)
        src = q_ref.at[:, hf, pl.ds(CROWS * k, CROWS), head_cols(j)]
        dst = qd.at[k, z]
        return src, dst, q_ss.at[0], q_rs.at[k, z], 4 * c + j, hf

    def b_send(j, hf):
        return bias_own, bias_all.at[z], b_ss.at[0], b_rs.at[0], 4 * c + j, hf

    def go(args):
        src, dst, ss, rs, d, hf = args
        mine = (d == z) & (c == hf)

        @pl.when(mine)
        def _():
            pltpu.make_async_copy(src, dst, rs).start()

        @pl.when(jnp.logical_not(mine))
        def _():
            remote(src, dst, ss, rs, at(y, d, x, hf)).start()

    def lag_slot(lag):
        return 16 + 7 - lag

    def relay_first(which, ahead):
        ref = (k_ref, v_ref)[which]
        return remote(
            ref.at[:, pl.ds(512, 128)], kv.at[lag_slot(7 if ahead else 1), which],
            rel_ss.at[0], rel_rs.at[ahead, 0],
            slot_dev(7 if ahead else 1),
        )

    def relay_next(step, ahead):
        old, new = (8 - step, 7 - step) if ahead else (step, step + 1)
        part = pl.ds(0, 512) if step < 3 else pl.ds(256 * ahead, 256)
        return remote(
            kv.at[lag_slot(old), :, part], kv.at[lag_slot(new), :, part],
            rel_ss.at[0], rel_rs.at[ahead, step],
            slot_dev(-1 if ahead else 1),
        )

    def send_kv(steps_of):
        for i in steps_of:
            for hf in range(2):
                for which in range(2):
                    go(kv_send(i, hf, which))

    def send_q(k):
        for i in range(4):
            for hf in range(2):
                go(q_send(i, hf, k))

    for ahead in range(2):
        for which in range(2):
            relay_first(which, ahead).start()
    send_kv((0, 1))
    for j in range(4):
        for hf in range(2):
            go(b_send(j, hf))
    w_send = remote(
        w_ref, wb.at[pl.ds(pl.multiple_of(c * WIDTH, 128), WIDTH)], w_ss.at[0], w_rs.at[0], twin
    )
    w_send.start()

    for copy in loads[:3]:
        copy.wait()

    def head_at_home(i, carry):
        head, half = i // 2, i % 2
        col = pl.ds(pl.multiple_of(head * 128, 128), 128)
        q = qv[pl.ds(2 * half, 2), :, :, col].reshape(256, HD)
        s = lax.dot_general(q, kvv[:, col], NT, preferred_element_type=jnp.float32)
        top = jnp.max(fold_max(s), axis=1, keepdims=True) * SCALE2
        p = jnp.exp2(s * SCALE2 - top)
        total = jnp.sum(fold_sum(p), axis=1, keepdims=True)
        o = jnp.dot(p.astype(jnp.bfloat16), vvv[:, col], preferred_element_type=jnp.float32)
        o0[pl.ds(2 * half, 2), :, :, col] = (
            (o / total).astype(jnp.bfloat16).reshape(2, 2, 64, HD)
        )
        return carry

    lax.fori_loop(0, 10, head_at_home, 0)
    own_cols = pl.ds(pl.multiple_of(c * WIDTH, 128), WIDTH)
    o0_own = pltpu.make_async_copy(o0.at[:, c], a0.at[:, :, own_cols], o0_sem.at[0])
    o0_twin = remote(
        o0.at[:, twin_c], a0.at[:, :, own_cols], o0_sem.at[1], o0_sem.at[2], twin
    )
    o0_own.start()
    o0_twin.start()

    half = pl.ds(pl.multiple_of(256 * c, 256), 256)
    other = pl.ds(pl.multiple_of(256 * twin_c, 256), 256)

    def to_twin(src_z):
        ref = kv.at[8 + src_z, :, half]
        return remote(ref, ref, ft_ss.at[0], ft_rs.at[0], twin)

    def to_next(src_z):
        return remote(
            kv.at[8 + src_z, :, half], kv.at[src_z, :, half], fy_ss.at[0],
            fy_rs.at[src_z], at(y + 1, z, x, c),
        )

    def prev_to_twin(src_z):
        ref = kv.at[src_z, :, half]
        return remote(ref, ref, fty_ss.at[0], fty_rs.at[src_z], twin)

    def pass_on(i):
        for far in range(2):
            src_z = lax.rem(z - i + NZ, 4) + 4 * far
            settle(kv.at[8 + src_z, :, half], kv_rs.at[src_z])
            pl.when(src_z > 0)(lambda: to_next(src_z).start())
            to_twin(src_z).start()

    def pass_prev(src_z):
        to_next(src_z).wait_recv()
        prev_to_twin(src_z).start()

    def relay(step):
        for ahead in range(2):
            if step == 1:
                settle(kv.at[lag_slot(7 if ahead else 1)], rel_rs.at[ahead, 0])
            else:
                relay_next(step - 1, ahead).wait_recv()
            if step < 4:
                relay_next(step, ahead).start()

    def half_cols(n, h):
        return pl.ds(pl.multiple_of(n * COLS + h * 512, 512), 512)

    def part_cols(n):
        return pl.ds(pl.multiple_of(n * COLS, COLS), COLS)

    right, left = lax.rem(x + 1, NX), lax.rem(x + 3, NX)
    opposite = lax.rem(x + 2, NX)

    def x_via(bufs, n, h):
        s_ref, r_ref, ss, rs = bufs
        ref = half_cols(n, h)
        return remote(
            s_ref.at[opposite, :, ref], r_ref.at[2, :, ref], ss, rs.at[n, 0],
            at(y, z, left if h else right, c),
        )

    def x_last(bufs, n, h):
        s_ref, r_ref, ss, rs = bufs
        to_x = left if h else right
        return remote(
            s_ref.at[to_x, :, part_cols(n)], r_ref.at[h, :, part_cols(n)], ss,
            rs.at[n, 1], at(y, z, to_x, c),
        )

    def add_on(bufs):
        lax.fori_loop(0, PARTS, functools.partial(add_part, bufs), 0)

    def add_part(bufs, n, carry):
        s_ref, r_ref, _, rs = bufs
        settle(r_ref.at[2, :, part_cols(n)], rs.at[n, 0])
        for h in range(2):
            to_x = left if h else right
            ref = half_cols(n, h)
            total = s_ref[to_x, :, ref].astype(jnp.float32) + r_ref[2, :, ref].astype(jnp.float32)
            s_ref[to_x, :, ref] = total.astype(jnp.bfloat16)
            x_last(bufs, n, h).start()
        return carry

    def project(a_ref, bufs, rows):
        s_ref = bufs[0]

        def part(n, carry):
            for h in range(2):
                col = half_cols(n, h)
                a = a_ref[...].reshape(NX * rows, 2 * WIDTH)
                out = jnp.dot(a, wb[:, col], preferred_element_type=jnp.float32)
                s_ref[:, :, col] = out.astype(jnp.bfloat16).reshape(NX, rows, 512)
                x_via(bufs, n, h).start()
            return carry

        lax.fori_loop(0, PARTS, part, 0)

    def gather_x(bufs, n, lat_rows, write):
        s_ref, r_ref, _, rs = bufs
        settle(r_ref.at[pl.ds(0, 2), :, part_cols(n)], rs.at[n, 1])
        for h in range(2):
            col = half_cols(n, h)
            total = s_ref[x, :, col].astype(jnp.float32)
            for i in range(2):
                total = total + r_ref[i, :, col].astype(jnp.float32)
            updated = lat[lat_rows, col].astype(jnp.float32) - gate_row[:, col] * total
            write(col, updated.astype(jnp.bfloat16))

    bufs0 = (s0, r0, x0_ss.at[0], x0_rs)
    bufs1 = [(s1.at[k], r1.at[k], x1_ss.at[k], x1_rs.at[k]) for k in range(CHUNKS)]

    for copy in loads[5:]:
        copy.wait()
    w_send.wait_recv()
    o0_own.wait()
    o0_twin.wait_recv()
    project(a0, bufs0, 64)

    relay(1)
    send_kv((2, 3))
    send_q(0)
    pass_on(0)
    pass_on(1)
    send_q(1)
    pass_on(2)
    add_on(bufs0)
    relay(2)
    pass_on(3)

    oldest = position == 0

    def write_u0(col, updated):
        u0[:, col] = jnp.where(oldest, updated, jnp.zeros_like(updated))

    def finish0(n, carry):
        gather_x(bufs0, n, slice(None), write_u0)
        return carry

    y_width = D // NY

    def y_send(dy):
        to_y = lax.rem(y + dy, NY)
        return remote(
            u0.at[:, pl.ds(pl.multiple_of(to_y * y_width, 128), y_width)], ry.at[3 - dy],
            y_ss.at[0], y_rs.at[0], at(to_y, z, x, c),
        )

    def finish_released():
        lax.fori_loop(0, PARTS, finish0, 0)
        for dy in range(1, NY):
            y_send(dy).start()

    def z_window(zz):
        return pl.ds(pl.multiple_of((zz * 160 // 128) * 128, 128), 256)

    def z_send(dz):
        to_z = lax.rem(z + dz, NZ)
        return remote(
            u1.at[:, z_window(to_z)], rz.at[7 - dz], z_ss.at[0], z_rs.at[0],
            at(y, to_z, x, c),
        )

    def share_y():
        settle(ry, y_rs.at[0])
        total = u0[:, pl.ds(pl.multiple_of(y * y_width, 128), y_width)].astype(jnp.float32)
        for i in range(3):
            total = total + ry[i].astype(jnp.float32)
        u1[...] = total.astype(jnp.bfloat16)
        for dz in range(1, NZ):
            z_send(dz).start()

    def share_z():
        settle(rz, z_rs.at[0])
        total = u1[:, z_window(z)].astype(jnp.float32)
        for i in range(7):
            total = total + rz[i].astype(jnp.float32)
        turned = pltpu.roll(total, lax.rem(256 - (z % 4) * 32, 256), 1)
        rel_ref[...] = turned[:, :160].astype(jnp.bfloat16)

    settle(kv.at[23], load_sem.at[3])
    settle(qd.at[:, pl.ds(8, 2)], load_sem.at[4])
    settle(bias_all.at[pl.ds(0, NZ)], b_rs.at[0])
    settle(kv.at[pl.ds(NZ, NZ), :, other], ft_rs.at[0])

    def item(it):
        stays = (it >= FIRST_STAY) & (it < FIRST_STAY + 4)
        order = jnp.where(it < FIRST_STAY, it, it - 4)
        k = jnp.where(stays, (it - FIRST_STAY) // 2, order // 8)
        gathered_s = 7 - order % 8
        s = jnp.where(stays, 8 + it % 2, gathered_s)
        return k, s, s, jnp.where(stays, 16, s + 1)

    def o_send(it):
        k, j, s, _ = item(it)
        gathered = j < 8
        to_z = jnp.where(gathered, s, z)
        to_c = jnp.where(gathered, c, j - 8)
        head_col = jnp.where(gathered, (z // 4) * WIDTH + (z % 4) * HD, c * WIDTH + 4 * HD)
        dst = a1.at[k, :, :, pl.ds(pl.multiple_of(head_col, 128), 128)]
        rs = o_rs.at[k]
        return os.at[k, s], dst, o_ss.at[0], rs, to_z, to_c

    def arrived(it):
        k, j, s, _ = item(it)
        pl.when(it == FIRST_STAY)(lambda: relay(4))

        @pl.when(j < 8)
        def _():
            settle(qd.at[k, s], q_rs.at[k, s])

        @pl.when((0 < s) & (s < 8) & (k == 0))
        def _():
            pass_prev(s)

        @pl.when((s < 7) & (k == 0))
        def _():
            prev_to_twin(s + 1).wait_recv()

    def first_pass(q, s, base, i, sc, top):
        scores = lax.dot_general(q, kv[base + i, 0], NT, preferred_element_type=jnp.float32)
        sc[i] = scores
        return jnp.maximum(top, fold_max(scores) * SCALE2 + bias_all[s, 7 - i : 8 - i, :])

    def second_pass(s, base, i, sc, top, total, acc):
        p = jnp.exp2(sc[i] * SCALE2 - lanes(top - bias_all[s, 7 - i : 8 - i, :], 512))
        acc = acc + jnp.dot(
            p.astype(jnp.bfloat16), kv[base + i, 1], preferred_element_type=jnp.float32
        )
        return total + fold_sum(p), acc

    def row_top(top):
        return jnp.broadcast_to(jnp.max(top, axis=1, keepdims=True), (M, HD))

    def stage(it, sc, m_ref, next_sc, next_m, last=False):
        k, j, s, base = item(it)
        if not last:
            arrived(it + 1)
            k2, _, s2, base2 = item(it + 1)
            q = qd[k2, s2].reshape(M, HD)
        top = m_ref[...]
        next_top = jnp.full((M, HD), FAR, jnp.float32)
        total = jnp.zeros((M, HD), jnp.float32)
        acc = jnp.zeros((M, HD), jnp.float32)
        for i in range(8):
            if not last:
                next_top = first_pass(q, s2, base2, i, next_sc, next_top)
            total, acc = second_pass(s, base, i, sc, top, total, acc)
        if not last:
            next_m[...] = row_top(next_top)
        o = acc / jnp.sum(total, axis=1, keepdims=True)
        os[k, s] = o.astype(jnp.bfloat16).reshape(NX, CROWS, HD)
        src, dst, ss, rs, to_z, to_c = o_send(it)
        mine = (to_z == z) & (to_c == c)

        @pl.when(mine)
        def _():
            pltpu.make_async_copy(src, dst, rs).start()

        @pl.when(jnp.logical_not(mine))
        def _():
            remote(src, dst, ss, rs, at(y, to_z, x, to_c)).start()

    def project_chunk(k):
        settle(a1.at[k], o_rs.at[k])
        project(a1.at[k], bufs1[k], CROWS)

    arrived(0)
    k, _, s, base = item(0)
    q = qd[k, s].reshape(M, HD)
    top = jnp.full((M, HD), FAR, jnp.float32)
    for i in range(8):
        top = first_pass(q, s, base, i, sca, top)
    ma[...] = row_top(top)

    steps = {
        "r1": lambda: relay(1), "r2": lambda: relay(2), "r3": lambda: relay(3),
        "r4": lambda: relay(4), "q1": lambda: send_q(1), "fr": finish_released,
        "sy": share_y, "sz": share_z, "p0": lambda: project_chunk(0),
    }

    def run(todo):
        for name in todo:
            steps[name]()

    def pair(j, carry):
        stage(2 * j, sca, ma, scb, mb)

        @pl.when(j < N_ITEMS // 2 - 1)
        def _():
            stage(2 * j + 1, scb, mb, sca, ma)

        for at_j, todo in PLAN.items():
            pl.when(j == at_j)(functools.partial(run, todo))

        return carry

    lax.fori_loop(0, N_ITEMS // 2, pair, 0)
    stage(N_ITEMS - 1, scb, mb, sca, ma, last=True)
    add_on(bufs1[0])
    project_chunk(1)
    share_y()
    add_on(bufs1[1])

    def out_copy(k, n):
        rows = pl.ds(CROWS * k, CROWS)
        return pltpu.make_async_copy(
            new.at[rows, part_cols(n)], out_ref.at[rows, part_cols(n)], out_sem.at[0]
        )

    def finish(k):
        rows = pl.ds(CROWS * k, CROWS)

        def write(col, updated):
            new[rows, col] = jnp.where(oldest, fre[rows, col], updated)

        def part(n, carry):
            gather_x(bufs1[k], n, rows, write)
            out_copy(k, n).start()
            return carry

        lax.fori_loop(0, PARTS, part, 0)

    finish(0)
    finish(1)
    share_z()
    pltpu.make_async_copy(new, out_ref, out_sem.at[0]).wait()

    def drain():
        has_own = z // 4 == c

        @pl.when(has_own)
        def _():
            settle(kv.at[pl.ds(0, 7), 0], kv_ss.at[0])
            settle(qd.at[:, pl.ds(0, 7)], q_ss.at[0])
            settle(bias_all.at[pl.ds(0, 7)], b_ss.at[0])

        @pl.when(jnp.logical_not(has_own))
        def _():
            settle(kv.at[pl.ds(0, 8), 0], kv_ss.at[0])
            settle(qd.at[:, pl.ds(0, 8)], q_ss.at[0])
            settle(bias_all.at[pl.ds(0, 8)], b_ss.at[0])

        settle(kv.at[pl.ds(0, 7)], rel_ss.at[0])
        w_send.wait_send()
        o0_twin.wait_send()
        settle(kv.at[pl.ds(0, 8), :, half], ft_ss.at[0])
        settle(kv.at[pl.ds(0, 7), :, half], fy_ss.at[0])
        settle(kv.at[pl.ds(0, 7), :, half], fty_ss.at[0])
        for bufs in [bufs0] + bufs1:
            settle(bufs[1], bufs[2])
        settle(ry, y_ss.at[0])
        settle(rz, z_ss.at[0])
        settle(os.at[:, pl.ds(0, 8)], o_ss.at[0])

    drain()


def body(
    latent, queries, keys, values, out_weight, level_gate, levels, offset, lag_mask, fresh_noise
):
    bf16, f32 = jnp.bfloat16, jnp.float32
    hbm = pl.BlockSpec(memory_space=pl.ANY)
    vmem = pl.BlockSpec(memory_space=pltpu.VMEM)
    smem = pl.BlockSpec(memory_space=pltpu.SMEM)
    dma = pltpu.SemaphoreType.DMA
    vm = pltpu.VMEM
    scratch = [
        vm((2 * WIDTH, D), bf16),
        vm((24, 2, ROWS, HD), bf16),
        vm((CHUNKS, ITEMS, NX, CROWS, HD), bf16),
        vm((ITEMS, 8, 128), f32),
        vm((CHUNKS, ITEMS, NX, CROWS, HD), bf16),
        vm((CHUNKS, NX, CROWS, 2 * WIDTH), bf16),
        vm((NX, 2, 64, WIDTH), bf16),
        vm((ROWS, WIDTH), bf16),
        vm((ROWS, WIDTH), bf16),
        vm((NX, 2, 64, WIDTH), bf16),
        vm((NX, 64, 2 * WIDTH), bf16),
        vm((NX, 64, D), bf16),
        vm((NX - 1, 64, D), bf16),
        vm((CHUNKS, NX, CROWS, D), bf16),
        vm((CHUNKS, NX - 1, CROWS, D), bf16),
        vm((64, D), bf16),
        vm((NY - 1, 64, D // NY), bf16),
        vm((64, D // NY), bf16),
        vm((NZ - 1, 64, 256), bf16),
        vm((64, D), bf16),
        vm((64, D), bf16),
        vm((64, D), bf16),
        vm((1, D), f32),
        vm((8, 128), f32),
        vm((8, M, ROWS), f32),
        vm((8, M, ROWS), f32),
        vm((M, HD), f32),
        vm((M, HD), f32),
        dma((8,)),
        dma((1,)), dma((NZ,)),
        dma((1,)), dma((2, 4)),
        dma((1,)), dma((CHUNKS, NZ)),
        dma((1,)), dma((1,)),
        dma((1,)), dma((1,)),
        dma((1,)), dma((1,)),
        dma((1,)), dma((NZ,)),
        dma((1,)), dma((NZ,)),
        dma((3,)),
        dma((1,)), dma((PARTS, 2)),
        dma((1,)), dma((CHUNKS,)),
        dma((CHUNKS,)), dma((CHUNKS, PARTS, 2)),
        dma((1,)),
        dma((1,)), dma((1,)),
        dma((1,)), dma((1,)),
    ]
    return pl.pallas_call(
        kernel,
        out_shape=(
            jax.ShapeDtypeStruct((64, D), bf16),
            jax.ShapeDtypeStruct((64, 160), bf16),
        ),
        in_specs=[hbm, hbm, hbm, hbm, hbm, vmem, smem, smem, smem, hbm],
        out_specs=(hbm, vmem),
        scratch_shapes=scratch,
        compiler_params=pltpu.CompilerParams(
            collective_id=1, has_side_effects=True, vmem_limit_bytes=56 << 20
        ),
        name="window_step",
    )(
        latent, queries.reshape(NX, 2, 64, WIDTH), keys, values, out_weight, level_gate,
        levels, offset, lag_mask, fresh_noise,
    )


def solution(mesh):
    return jax.shard_map(
        body,
        mesh=mesh,
        in_specs=(
            P(("span", "tp"), None),
            P("span", "tp"),
            P("span", "tp"),
            P("span", "tp"),
            P("tp", None),
            P(),
            P("span"),
            P(),
            P("span", None),
            P("tp", None),
        ),
        out_specs=(P(("span", "tp"), None), P("tp", "span")),
        check_vma=False,
    )
```

```python
import functools

import jax
import jax.numpy as jnp
from jax import lax
from jax.experimental import pallas as pl
from jax.experimental.pallas import tpu as pltpu
from jax.sharding import PartitionSpec as P

MESH = pl.DeviceIdType.MESH
HD = 128
ROWS = 512
WIDTH = 640
D = 5120
NY, NZ, NX = 4, 8, 4
SLOTS = NY * NZ
LAGS = 7
CHUNKS = 2
CROWS = 64 // CHUNKS
M = NX * CROWS
ITEMS = 10
N_ITEMS = CHUNKS * ITEMS
FAR = -1e30
SCALE2 = HD ** -0.5 * 1.4426950408889634
COLS = 1024
PARTS = D // COLS
NT = (((1,), (1,)), ((), ()))
FIRST_STAY = 14
PLAN = {1: ("r3",), 5: ("fr",), 8: ("p0",)}


def lanes(col, width):
    return jnp.concatenate([col] * (width // HD), axis=1)


def fold_max(x):
    return jnp.maximum(
        jnp.maximum(x[:, :128], x[:, 128:256]), jnp.maximum(x[:, 256:384], x[:, 384:])
    )


def fold_sum(x):
    return (x[:, :128] + x[:, 128:256]) + (x[:, 256:384] + x[:, 384:])


def kernel(
    latent_ref, q_ref, k_ref, v_ref, w_ref, gate_ref, levels_ref, offset_ref, mask_ref,
    fresh_ref, out_ref, rel_ref,
    wb, kv, qd, bias_all, os, a1, qv, kvv, vvv, o0, a0, s0, r0, s1, r1, u0, ry, u1, rz,
    new, lat, fre, gate_row, bias_own, sca, scb, ma, mb,
    load_sem, kv_ss, kv_rs, rel_ss, rel_rs, q_ss, q_rs, b_ss, b_rs, w_ss, w_rs,
    ft_ss, ft_rs, fy_ss, fy_rs, fty_ss, fty_rs, o0_sem, x0_ss, x0_rs, o_ss, o_rs,
    x1_ss, x1_rs, out_sem, y_ss, y_rs, z_ss, z_rs,
):
    me = lax.axis_index("span")
    t = lax.axis_index("tp")
    y, z = me // NZ, me % NZ
    x, c = t // 2, t % 2
    twin_c = 1 - c

    def at(yy, zz, xx, cc):
        return (lax.rem(yy + NY, NY) * NZ + lax.rem(zz + NZ, NZ), lax.rem(xx + NX, NX) * 2 + cc)

    def slot_dev(shift):
        return (lax.rem(me + shift + SLOTS, SLOTS), t)

    twin = at(y, z, x, twin_c)

    def remote(src, dst, ss, rs, dev):
        return pltpu.make_async_remote_copy(
            src_ref=src, dst_ref=dst, send_sem=ss, recv_sem=rs, device_id=dev,
            device_id_type=MESH,
        )

    def settle(ref, sem):
        pltpu.make_async_copy(ref, ref, sem).wait()

    loads = [
        pltpu.make_async_copy(q_ref, qv, load_sem.at[0]),
        pltpu.make_async_copy(k_ref, kvv, load_sem.at[1]),
        pltpu.make_async_copy(v_ref, vvv, load_sem.at[2]),
        pltpu.make_async_copy(k_ref.at[:, pl.ds(512, 128)], kv.at[23, 0], load_sem.at[3]),
        pltpu.make_async_copy(v_ref.at[:, pl.ds(512, 128)], kv.at[23, 1], load_sem.at[3]),
        pltpu.make_async_copy(
            w_ref, wb.at[pl.ds(pl.multiple_of(c * WIDTH, 128), WIDTH)], load_sem.at[5]
        ),
        pltpu.make_async_copy(latent_ref, lat, load_sem.at[6]),
        pltpu.make_async_copy(fresh_ref, fre, load_sem.at[7]),
    ]
    for copy in loads:
        copy.start()
    q_loads = []
    for k in range(CHUNKS):
        for p in range(2):
            q_loads.append(
                pltpu.make_async_copy(
                    q_ref.at[:, p, pl.ds(CROWS * k, CROWS), pl.ds(512, 128)],
                    qd.at[k, 8 + p], load_sem.at[4],
                )
            )
            q_loads[-1].start()

    barrier = pltpu.get_barrier_semaphore()
    partners = [twin]
    for dz in range(1, NZ):
        partners += [at(y, z + dz, x, c), at(y, z + dz, x, twin_c)]
    for dy in range(1, NY):
        partners.append(at(y + dy, z, x, c))
    for dx in range(1, NX):
        partners.append(at(y, z, x + dx, c))
    for shift in (1, -1, 7, -7):
        partners.append(slot_dev(shift))
    for dev in partners:
        pl.semaphore_signal(barrier, inc=1, device_id=dev, device_id_type=MESH)
    pl.semaphore_wait(barrier, len(partners))

    position = lax.rem(me - offset_ref[0] + SLOTS, SLOTS)
    lag_at = lax.broadcasted_iota(jnp.int32, (8, 128), 0)
    bias = jnp.zeros((8, 128), jnp.float32)
    for lag in range(1, LAGS + 1):
        ok = (mask_ref[0, lag - 1] == 1) & (position >= lag)
        bias = jnp.where(lag_at == lag, jnp.where(ok, 0.0, FAR), bias)
    bias_own[...] = bias
    bias_all[8] = bias
    bias_all[9] = bias
    level = levels_ref[0]
    row = gate_ref[0:1, :]
    for i in range(1, 4):
        row = jnp.where(level == i, gate_ref[i : i + 1, :], row)
    gate_row[...] = row * 0.25

    def turned(i):
        return lax.rem(z + i, 4)

    def head_cols(j):
        return pl.ds(pl.multiple_of(128 * j, 128), 128)

    def kv_send(i, hf, which):
        j = turned(i)
        ref = (k_ref, v_ref)[which]
        src = ref.at[pl.ds(256 * hf, 256), head_cols(j)]
        dst = kv.at[8 + z, which, pl.ds(256 * hf, 256)]
        d = 4 * c + j
        return src, dst, kv_ss.at[0], kv_rs.at[z], d, hf

    def q_send(i, hf, k):
        j = turned(i)
        src = q_ref.at[:, hf, pl.ds(CROWS * k, CROWS), head_cols(j)]
        dst = qd.at[k, z]
        return src, dst, q_ss.at[0], q_rs.at[k, z], 4 * c + j, hf

    def b_send(j, hf):
        return bias_own, bias_all.at[z], b_ss.at[0], b_rs.at[0], 4 * c + j, hf

    def go(args):
        src, dst, ss, rs, d, hf = args
        mine = (d == z) & (c == hf)

        @pl.when(mine)
        def _():
            pltpu.make_async_copy(src, dst, rs).start()

        @pl.when(jnp.logical_not(mine))
        def _():
            remote(src, dst, ss, rs, at(y, d, x, hf)).start()

    def lag_slot(lag):
        return 16 + 7 - lag

    def relay_first(which, ahead):
        ref = (k_ref, v_ref)[which]
        return remote(
            ref.at[:, pl.ds(512, 128)], kv.at[lag_slot(7 if ahead else 1), which],
            rel_ss.at[0], rel_rs.at[ahead, 0],
            slot_dev(7 if ahead else 1),
        )

    def relay_next(step, ahead):
        old, new = (8 - step, 7 - step) if ahead else (step, step + 1)
        part = pl.ds(0, 512) if step < 3 else pl.ds(256 * ahead, 256)
        return remote(
            kv.at[lag_slot(old), :, part], kv.at[lag_slot(new), :, part],
            rel_ss.at[0], rel_rs.at[ahead, step],
            slot_dev(-1 if ahead else 1),
        )

    def send_kv(steps_of):
        for i in steps_of:
            for hf in range(2):
                for which in range(2):
                    go(kv_send(i, hf, which))

    def send_q(k):
        for i in range(4):
            for hf in range(2):
                go(q_send(i, hf, k))

    for ahead in range(2):
        for which in range(2):
            relay_first(which, ahead).start()
    send_kv((0, 1))
    for j in range(4):
        for hf in range(2):
            go(b_send(j, hf))
    w_send = remote(
        w_ref, wb.at[pl.ds(pl.multiple_of(c * WIDTH, 128), WIDTH)], w_ss.at[0], w_rs.at[0], twin
    )
    w_send.start()

    for copy in loads[:3]:
        copy.wait()

    def head_at_home(i, carry):
        head, half = i // 2, i % 2
        col = pl.ds(pl.multiple_of(head * 128, 128), 128)
        q = qv[pl.ds(2 * half, 2), :, :, col].reshape(256, HD)
        s = lax.dot_general(q, kvv[:, col], NT, preferred_element_type=jnp.float32)
        top = jnp.max(fold_max(s), axis=1, keepdims=True) * SCALE2
        p = jnp.exp2(s * SCALE2 - top)
        total = jnp.sum(fold_sum(p), axis=1, keepdims=True)
        o = jnp.dot(p.astype(jnp.bfloat16), vvv[:, col], preferred_element_type=jnp.float32)
        o0[pl.ds(2 * half, 2), :, :, col] = (
            (o / total).astype(jnp.bfloat16).reshape(2, 2, 64, HD)
        )
        return carry

    lax.fori_loop(0, 10, head_at_home, 0)
    own_cols = pl.ds(pl.multiple_of(c * WIDTH, 128), WIDTH)
    o0_own = pltpu.make_async_copy(o0.at[:, c], a0.at[:, :, own_cols], o0_sem.at[0])
    o0_twin = remote(
        o0.at[:, twin_c], a0.at[:, :, own_cols], o0_sem.at[1], o0_sem.at[2], twin
    )
    o0_own.start()
    o0_twin.start()

    half = pl.ds(pl.multiple_of(256 * c, 256), 256)
    other = pl.ds(pl.multiple_of(256 * twin_c, 256), 256)

    def to_twin(src_z):
        ref = kv.at[8 + src_z, :, half]
        return remote(ref, ref, ft_ss.at[0], ft_rs.at[0], twin)

    def to_next(src_z):
        return remote(
            kv.at[8 + src_z, :, half], kv.at[src_z, :, half], fy_ss.at[0],
            fy_rs.at[src_z], at(y + 1, z, x, c),
        )

    def prev_to_twin(src_z):
        ref = kv.at[src_z, :, half]
        return remote(ref, ref, fty_ss.at[0], fty_rs.at[src_z], twin)

    def pass_on(i):
        for far in range(2):
            src_z = lax.rem(z - i + NZ, 4) + 4 * far
            settle(kv.at[8 + src_z, :, half], kv_rs.at[src_z])
            pl.when(src_z > 0)(lambda: to_next(src_z).start())
            to_twin(src_z).start()

    def pass_prev(src_z):
        to_next(src_z).wait_recv()
        prev_to_twin(src_z).start()

    def relay(step):
        for ahead in range(2):
            if step == 1:
                settle(kv.at[lag_slot(7 if ahead else 1)], rel_rs.at[ahead, 0])
            else:
                relay_next(step - 1, ahead).wait_recv()
            if step < 4:
                relay_next(step, ahead).start()

    def half_cols(n, h):
        return pl.ds(pl.multiple_of(n * COLS + h * 512, 512), 512)

    def part_cols(n):
        return pl.ds(pl.multiple_of(n * COLS, COLS), COLS)

    right, left = lax.rem(x + 1, NX), lax.rem(x + 3, NX)
    opposite = lax.rem(x + 2, NX)

    def x_via(bufs, n, h):
        s_ref, r_ref, ss, rs = bufs
        ref = half_cols(n, h)
        return remote(
            s_ref.at[opposite, :, ref], r_ref.at[2, :, ref], ss, rs.at[n, 0],
            at(y, z, left if h else right, c),
        )

    def x_last(bufs, n, h):
        s_ref, r_ref, ss, rs = bufs
        to_x = left if h else right
        return remote(
            s_ref.at[to_x, :, part_cols(n)], r_ref.at[h, :, part_cols(n)], ss,
            rs.at[n, 1], at(y, z, to_x, c),
        )

    def add_on(bufs):
        lax.fori_loop(0, PARTS, functools.partial(add_part, bufs), 0)

    def add_part(bufs, n, carry):
        s_ref, r_ref, _, rs = bufs
        settle(r_ref.at[2, :, part_cols(n)], rs.at[n, 0])
        for h in range(2):
            to_x = left if h else right
            ref = half_cols(n, h)
            total = s_ref[to_x, :, ref].astype(jnp.float32) + r_ref[2, :, ref].astype(jnp.float32)
            s_ref[to_x, :, ref] = total.astype(jnp.bfloat16)
            x_last(bufs, n, h).start()
        return carry

    def project(a_ref, bufs, rows):
        s_ref = bufs[0]

        def part(n, carry):
            for h in range(2):
                col = half_cols(n, h)
                a = a_ref[...].reshape(NX * rows, 2 * WIDTH)
                out = jnp.dot(a, wb[:, col], preferred_element_type=jnp.float32)
                s_ref[:, :, col] = out.astype(jnp.bfloat16).reshape(NX, rows, 512)
                x_via(bufs, n, h).start()
            return carry

        lax.fori_loop(0, PARTS, part, 0)

    def gather_x(bufs, n, lat_rows, write):
        s_ref, r_ref, _, rs = bufs
        settle(r_ref.at[pl.ds(0, 2), :, part_cols(n)], rs.at[n, 1])
        for h in range(2):
            col = half_cols(n, h)
            total = s_ref[x, :, col].astype(jnp.float32)
            for i in range(2):
                total = total + r_ref[i, :, col].astype(jnp.float32)
            updated = lat[lat_rows, col].astype(jnp.float32) - gate_row[:, col] * total
            write(col, updated.astype(jnp.bfloat16))

    bufs0 = (s0, r0, x0_ss.at[0], x0_rs)
    bufs1 = [(s1.at[k], r1.at[k], x1_ss.at[k], x1_rs.at[k]) for k in range(CHUNKS)]

    for copy in loads[5:]:
        copy.wait()
    w_send.wait_recv()
    o0_own.wait()
    o0_twin.wait_recv()
    project(a0, bufs0, 64)

    relay(1)
    send_kv((2, 3))
    send_q(0)
    pass_on(0)
    pass_on(1)
    send_q(1)
    pass_on(2)
    add_on(bufs0)
    relay(2)
    pass_on(3)

    oldest = position == 0

    def write_u0(col, updated):
        u0[:, col] = jnp.where(oldest, updated, jnp.zeros_like(updated))

    def finish0(n, carry):
        gather_x(bufs0, n, slice(None), write_u0)
        return carry

    y_width = D // NY

    def y_send(dy):
        to_y = lax.rem(y + dy, NY)
        return remote(
            u0.at[:, pl.ds(pl.multiple_of(to_y * y_width, 128), y_width)], ry.at[3 - dy],
            y_ss.at[0], y_rs.at[0], at(to_y, z, x, c),
        )

    def finish_released():
        lax.fori_loop(0, PARTS, finish0, 0)
        for dy in range(1, NY):
            y_send(dy).start()

    def z_window(zz):
        return pl.ds(pl.multiple_of((zz * 160 // 128) * 128, 128), 256)

    def z_send(dz):
        to_z = lax.rem(z + dz, NZ)
        return remote(
            u1.at[:, z_window(to_z)], rz.at[7 - dz], z_ss.at[0], z_rs.at[0],
            at(y, to_z, x, c),
        )

    def share_y():
        settle(ry, y_rs.at[0])
        total = u0[:, pl.ds(pl.multiple_of(y * y_width, 128), y_width)].astype(jnp.float32)
        for i in range(3):
            total = total + ry[i].astype(jnp.float32)
        u1[...] = total.astype(jnp.bfloat16)
        for dz in range(1, NZ):
            z_send(dz).start()

    def share_z():
        settle(rz, z_rs.at[0])
        total = u1[:, z_window(z)].astype(jnp.float32)
        for i in range(7):
            total = total + rz[i].astype(jnp.float32)
        turned = pltpu.roll(total, lax.rem(256 - (z % 4) * 32, 256), 1)
        rel_ref[...] = turned[:, :160].astype(jnp.bfloat16)

    settle(kv.at[23], load_sem.at[3])
    settle(qd.at[:, pl.ds(8, 2)], load_sem.at[4])
    settle(bias_all.at[pl.ds(0, NZ)], b_rs.at[0])
    settle(kv.at[pl.ds(NZ, NZ), :, other], ft_rs.at[0])

    def item(it):
        stays = (it >= FIRST_STAY) & (it < FIRST_STAY + 4)
        order = jnp.where(it < FIRST_STAY, it, it - 4)
        k = jnp.where(stays, (it - FIRST_STAY) // 2, order // 8)
        gathered_s = 7 - order % 8
        s = jnp.where(stays, 8 + it % 2, gathered_s)
        return k, s, s, jnp.where(stays, 16, s + 1)

    def o_send(it):
        k, j, s, _ = item(it)
        gathered = j < 8
        to_z = jnp.where(gathered, s, z)
        to_c = jnp.where(gathered, c, j - 8)
        head_col = jnp.where(gathered, (z // 4) * WIDTH + (z % 4) * HD, c * WIDTH + 4 * HD)
        dst = a1.at[k, :, :, pl.ds(pl.multiple_of(head_col, 128), 128)]
        rs = o_rs.at[k]
        return os.at[k, s], dst, o_ss.at[0], rs, to_z, to_c

    def arrived(it):
        k, j, s, _ = item(it)
        pl.when(it == FIRST_STAY)(lambda: relay(4))

        @pl.when(j < 8)
        def _():
            settle(qd.at[k, s], q_rs.at[k, s])

        @pl.when((0 < s) & (s < 8) & (k == 0))
        def _():
            pass_prev(s)

        @pl.when((s < 7) & (k == 0))
        def _():
            prev_to_twin(s + 1).wait_recv()

    def first_pass(q, s, base, i, sc, top):
        scores = lax.dot_general(q, kv[base + i, 0], NT, preferred_element_type=jnp.float32)
        sc[i] = scores
        return jnp.maximum(top, fold_max(scores) * SCALE2 + bias_all[s, 7 - i : 8 - i, :])

    def second_pass(s, base, i, sc, top, total, acc):
        p = jnp.exp2(sc[i] * SCALE2 - lanes(top - bias_all[s, 7 - i : 8 - i, :], 512))
        acc = acc + jnp.dot(
            p.astype(jnp.bfloat16), kv[base + i, 1], preferred_element_type=jnp.float32
        )
        return total + fold_sum(p), acc

    def row_top(top):
        return jnp.broadcast_to(jnp.max(top, axis=1, keepdims=True), (M, HD))

    def stage(it, sc, m_ref, next_sc, next_m, last=False):
        k, j, s, base = item(it)
        if not last:
            arrived(it + 1)
            k2, _, s2, base2 = item(it + 1)
            q = qd[k2, s2].reshape(M, HD)
        top = m_ref[...]
        next_top = jnp.full((M, HD), FAR, jnp.float32)
        total = jnp.zeros((M, HD), jnp.float32)
        acc = jnp.zeros((M, HD), jnp.float32)
        for i in range(8):
            if not last:
                next_top = first_pass(q, s2, base2, i, next_sc, next_top)
            total, acc = second_pass(s, base, i, sc, top, total, acc)
        if not last:
            next_m[...] = row_top(next_top)
        o = acc / jnp.sum(total, axis=1, keepdims=True)
        os[k, s] = o.astype(jnp.bfloat16).reshape(NX, CROWS, HD)
        src, dst, ss, rs, to_z, to_c = o_send(it)
        mine = (to_z == z) & (to_c == c)

        @pl.when(mine)
        def _():
            pltpu.make_async_copy(src, dst, rs).start()

        @pl.when(jnp.logical_not(mine))
        def _():
            remote(src, dst, ss, rs, at(y, to_z, x, to_c)).start()

    def project_chunk(k):
        settle(a1.at[k], o_rs.at[k])
        project(a1.at[k], bufs1[k], CROWS)

    arrived(0)
    k, _, s, base = item(0)
    q = qd[k, s].reshape(M, HD)
    top = jnp.full((M, HD), FAR, jnp.float32)
    for i in range(8):
        top = first_pass(q, s, base, i, sca, top)
    ma[...] = row_top(top)

    steps = {
        "r1": lambda: relay(1), "r2": lambda: relay(2), "r3": lambda: relay(3),
        "r4": lambda: relay(4), "q1": lambda: send_q(1), "fr": finish_released,
        "sy": share_y, "sz": share_z, "p0": lambda: project_chunk(0),
    }

    def run(todo):
        for name in todo:
            steps[name]()

    def pair(j, carry):
        stage(2 * j, sca, ma, scb, mb)

        @pl.when(j < N_ITEMS // 2 - 1)
        def _():
            stage(2 * j + 1, scb, mb, sca, ma)

        for at_j, todo in PLAN.items():
            pl.when(j == at_j)(functools.partial(run, todo))

        return carry

    lax.fori_loop(0, N_ITEMS // 2, pair, 0)
    stage(N_ITEMS - 1, scb, mb, sca, ma, last=True)
    add_on(bufs1[0])
    project_chunk(1)
    share_y()
    add_on(bufs1[1])

    def out_copy(k, n):
        rows = pl.ds(CROWS * k, CROWS)
        return pltpu.make_async_copy(
            new.at[rows, part_cols(n)], out_ref.at[rows, part_cols(n)], out_sem.at[0]
        )

    def finish(k):
        rows = pl.ds(CROWS * k, CROWS)

        def write(col, updated):
            new[rows, col] = jnp.where(oldest, fre[rows, col], updated)

        def part(n, carry):
            gather_x(bufs1[k], n, rows, write)
            out_copy(k, n).start()
            return carry

        lax.fori_loop(0, PARTS, part, 0)

    finish(0)
    finish(1)
    share_z()
    pltpu.make_async_copy(new, out_ref, out_sem.at[0]).wait()

    def drain():
        has_own = z // 4 == c

        @pl.when(has_own)
        def _():
            settle(kv.at[pl.ds(0, 7), 0], kv_ss.at[0])
            settle(qd.at[:, pl.ds(0, 7)], q_ss.at[0])
            settle(bias_all.at[pl.ds(0, 7)], b_ss.at[0])

        @pl.when(jnp.logical_not(has_own))
        def _():
            settle(kv.at[pl.ds(0, 8), 0], kv_ss.at[0])
            settle(qd.at[:, pl.ds(0, 8)], q_ss.at[0])
            settle(bias_all.at[pl.ds(0, 8)], b_ss.at[0])

        settle(kv.at[pl.ds(0, 7)], rel_ss.at[0])
        w_send.wait_send()
        o0_twin.wait_send()
        settle(kv.at[pl.ds(0, 8), :, half], ft_ss.at[0])
        settle(kv.at[pl.ds(0, 7), :, half], fy_ss.at[0])
        settle(kv.at[pl.ds(0, 7), :, half], fty_ss.at[0])
        for bufs in [bufs0] + bufs1:
            settle(bufs[1], bufs[2])
        settle(ry, y_ss.at[0])
        settle(rz, z_ss.at[0])
        settle(os.at[:, pl.ds(0, 8)], o_ss.at[0])

    drain()


def hand_over(next_in, rel_in, next_out, rel_out):
    next_out[...] = next_in[...]
    rel_out[...] = rel_in[...]


def body(
    latent, queries, keys, values, out_weight, level_gate, levels, offset, lag_mask, fresh_noise
):
    bf16, f32 = jnp.bfloat16, jnp.float32
    hbm = pl.BlockSpec(memory_space=pl.ANY)
    vmem = pl.BlockSpec(memory_space=pltpu.VMEM)
    smem = pl.BlockSpec(memory_space=pltpu.SMEM)
    dma = pltpu.SemaphoreType.DMA
    vm = pltpu.VMEM
    scratch = [
        vm((2 * WIDTH, D), bf16),
        vm((24, 2, ROWS, HD), bf16),
        vm((CHUNKS, ITEMS, NX, CROWS, HD), bf16),
        vm((ITEMS, 8, 128), f32),
        vm((CHUNKS, ITEMS, NX, CROWS, HD), bf16),
        vm((CHUNKS, NX, CROWS, 2 * WIDTH), bf16),
        vm((NX, 2, 64, WIDTH), bf16),
        vm((ROWS, WIDTH), bf16),
        vm((ROWS, WIDTH), bf16),
        vm((NX, 2, 64, WIDTH), bf16),
        vm((NX, 64, 2 * WIDTH), bf16),
        vm((NX, 64, D), bf16),
        vm((NX - 1, 64, D), bf16),
        vm((CHUNKS, NX, CROWS, D), bf16),
        vm((CHUNKS, NX - 1, CROWS, D), bf16),
        vm((64, D), bf16),
        vm((NY - 1, 64, D // NY), bf16),
        vm((64, D // NY), bf16),
        vm((NZ - 1, 64, 256), bf16),
        vm((64, D), bf16),
        vm((64, D), bf16),
        vm((64, D), bf16),
        vm((1, D), f32),
        vm((8, 128), f32),
        vm((8, M, ROWS), f32),
        vm((8, M, ROWS), f32),
        vm((M, HD), f32),
        vm((M, HD), f32),
        dma((8,)),
        dma((1,)), dma((NZ,)),
        dma((1,)), dma((2, 4)),
        dma((1,)), dma((CHUNKS, NZ)),
        dma((1,)), dma((1,)),
        dma((1,)), dma((1,)),
        dma((1,)), dma((1,)),
        dma((1,)), dma((NZ,)),
        dma((1,)), dma((NZ,)),
        dma((3,)),
        dma((1,)), dma((PARTS, 2)),
        dma((1,)), dma((CHUNKS,)),
        dma((CHUNKS,)), dma((CHUNKS, PARTS, 2)),
        dma((1,)),
        dma((1,)), dma((1,)),
        dma((1,)), dma((1,)),
    ]
    made = pl.pallas_call(
        kernel,
        out_shape=(
            jax.ShapeDtypeStruct((64, D), bf16),
            jax.ShapeDtypeStruct((64, 160), bf16),
        ),
        in_specs=[hbm, hbm, hbm, hbm, hbm, vmem, smem, smem, smem, hbm],
        out_specs=(hbm, vmem),
        scratch_shapes=scratch,
        compiler_params=pltpu.CompilerParams(
            collective_id=1, has_side_effects=True, vmem_limit_bytes=56 << 20
        ),
        name="window_step",
    )(
        latent, queries.reshape(NX, 2, 64, WIDTH), keys, values, out_weight, level_gate,
        levels, offset, lag_mask, fresh_noise,
    )
    return pl.pallas_call(
        hand_over,
        out_shape=tuple(jax.ShapeDtypeStruct(a.shape, a.dtype) for a in made),
        in_specs=[vmem, vmem],
        out_specs=(vmem, vmem),
        name="hand_over",
    )(*made)


def solution(mesh):
    return jax.shard_map(
        body,
        mesh=mesh,
        in_specs=(
            P(("span", "tp"), None),
            P("span", "tp"),
            P("span", "tp"),
            P("span", "tp"),
            P("tp", None),
            P(),
            P("span"),
            P(),
            P("span", None),
            P("tp", None),
        ),
        out_specs=(P(("span", "tp"), None), P("tp", "span")),
        check_vma=False,
    )
```
